512 devices in a mesh: shard: 8 (over x, core), grp: 64 (over z, y).
Axes of the slice: x: 4, y: 4, z: 16, core: 2. Of those that a mesh axis runs over, the one named last changes fastest.
Arguments:
- embeddings: bfloat16 [131072, 768], P(('shard', 'grp')), parts along dimension 0, may hold values from -6 to 6
- cluster_ids: int32 [131072, 1], P(('shard', 'grp')), parts along dimension 0, may hold values from 0 to 127; in each aligned block of 256 rows (0 to 255, 256 to 511, ...) at most 4 rows name the same one
- ranks: int32 [131072], P(('shard', 'grp')), parts along dimension 0, may hold values from 0 to 16383, each once
Outputs:
- best_sim: float32 [131072], P(('shard', 'grp')), parts along dimension 0
The draws below stay inside these ranges and needn't reach their ends.
There are 8 independent parts, one for each index of `shard`. The reference program is written for one: setup_inputs(seed, part) draws one part's arguments, and reference() takes and returns one part's arrays. A program takes and returns all parts, laid end to end along the dimension named above; each array names one. Nothing has to cross between parts.
Inputs may be any that keep to these rules, and one draw needn't show every extreme that they name: `cluster_ids`: among the rows of one device no cluster is named by more than 4 rows, a bound that some block reaches. `ranks`: every value occurs once.
All inputs are finite; a program needn't handle non-finite values.
Results may differ from the reference program's by a relative error of at most 0.0013.
Values may be sent and summed in bfloat16 or wider, within the bound.
No kernel may reach another device: no remote copies, remote signals or barrier semaphores. Data moves between devices by JAX's collectives and lax.ppermute only.
A program may use at most 64 MiB of HBM per device.

```python
import math
import jax
import jax.numpy as jnp
import numpy as np
from jax import lax

D = 768
ROWS_DEV = 256
CLUSTERS = 128
SLOT = 4
ROWS_ALL = 16384
N_GRP = 64


def levels(stream_key, extent, shards, least, top_value):
    factor_of = 1.0
    for dim, shards_of in shards:
        draws = jax.random.uniform(jax.random.fold_in(jax.random.fold_in(stream_key, 6), dim), (shards_of,), jnp.float32, least / len(shards), top_value / len(shards))
        factor_of = factor_of * jnp.repeat(jnp.exp(draws), extent[dim] // shards_of).reshape((-1,) + (1,) * (len(extent) - 1 - dim))
    return factor_of


def deal_out(own_key, own, number, rows, number_of, top, most, slope):
    ranking = jax.random.permutation(own_key, number_of)
    heavy_load, usual = shares(number_of, rows * top, most, slope, True), shares(number_of, rows * top, most, slope, False)
    places = jnp.arange(number_of)

    def named(lengths, rotation):
        used = int((lengths > 0).sum())
        fixed = max(1, used // 4)
        moved = fixed + (places - fixed + rotation * (used - fixed)) % max(1, number_of - fixed)
        return jnp.zeros((number_of,), jnp.int32).at[ranking[jnp.where(places < fixed, places, moved)]].set(jnp.asarray(lengths, jnp.int32))

    lengths = jnp.where(number % 4 == 0, named(heavy_load, number // 4), named(usual, number - number // 4 - 1))
    mixed = jax.random.permutation(jax.random.fold_in(own, 3), number_of)
    giver, receiver = mixed[0:number_of // 2 * 2:2], mixed[1:number_of // 2 * 2:2]
    margin = jnp.minimum(lengths[giver] - 1, most - lengths[receiver]) // 2
    margin = jnp.where((giver == ranking[0]) | (receiver == ranking[0]) | (lengths[receiver] == 0), 0, jnp.maximum(margin, 0))
    moved = jax.random.randint(jax.random.fold_in(own, 4), (number_of // 2,), 0, 1 << 20) % (margin + 1)
    lengths = lengths.at[giver].add(-moved).at[receiver].add(moved)
    members = jnp.searchsorted(jnp.cumsum(lengths), jnp.arange(rows * top), side="right").astype(jnp.int32)
    listing = members.reshape(top, rows).T
    listing = listing[jax.random.permutation(jax.random.fold_in(own, 1), rows)]
    rotation = jax.random.randint(jax.random.fold_in(own, 2), (rows, 1), 0, top)
    return jnp.take_along_axis(listing, (jnp.arange(top)[None, :] + rotation) % top, axis=1)


def shares(count, total, limit, skew, full):
    loads = [(1 << 20) // math.isqrt(standing ** skew) + 1 for standing in range(1, count + 1)]
    largest = limit if full else min(limit, max(-(-total // count), total * loads[0] // sum(loads)))
    least = 1 if total - largest >= count - 1 else 0
    holding, spare = [largest] + [least] * (count - 1), total - largest - least * (count - 1)
    while spare > 0:
        movable = [i for i in range(1, count) if holding[i] < largest] or [i for i in range(1, count) if holding[i] < limit]
        whole, left = sum([loads[i] for i in movable]), spare
        for i in movable:
            more = min(limit - holding[i], max(1, left * loads[i] // whole), spare)
            holding[i] = holding[i] + more
            spare = spare - more
    return np.array(holding)


def gaussian(key, shape, spread, bound, cuts=(), kind=jnp.bfloat16):
    factor_of = levels(key, shape, cuts, -0.22, 0.18) if cuts else 1.0
    entries = jax.random.normal(key, shape, jnp.float32) * spread * factor_of
    return jnp.minimum(jnp.maximum(entries, -bound), bound).astype(kind)


def setup_inputs(seed: int = 0, part: int = 0) -> dict:
    seeds = jax.random.split(jax.random.key(seed), 4)
    part_splits = jax.random.split(jax.random.fold_in(seeds[3], part), 4)
    embeddings = gaussian(part_splits[0], (ROWS_ALL, D), 1.0, 6.0, ((0, 64),))
    cluster_ids_keys = jax.random.split(jax.random.fold_in(part_splits[1], 1), ROWS_ALL // ROWS_DEV)
    cluster_ids_turns = jax.random.permutation(jax.random.fold_in(part_splits[1], 3), ROWS_ALL // ROWS_DEV)
    cluster_ids = jax.vmap(lambda own, number: deal_out(jax.random.fold_in(part_splits[1], 2), own, number, ROWS_DEV, CLUSTERS, 1, SLOT, 2))(cluster_ids_keys, cluster_ids_turns).reshape((ROWS_ALL, 1))
    ranks = jax.random.permutation(part_splits[2], ROWS_ALL).astype(jnp.int32)
    return dict(embeddings=embeddings, cluster_ids=cluster_ids, ranks=ranks)


def reference(embeddings, cluster_ids, ranks):
    floats = embeddings.astype(jnp.float32)
    unit_rows = (floats * lax.rsqrt(lax.optimization_barrier(jnp.sum(floats * floats, axis=1, keepdims=True)) + 1e-06)).astype(jnp.bfloat16)
    cluster_of = cluster_ids[:, 0].astype(jnp.int32)
    sort_key = cluster_of * ROWS_ALL + ranks.astype(jnp.int32)
    sort_order = jnp.argsort(sort_key).astype(jnp.int32)
    sorted_rows = unit_rows[sort_order].astype(jnp.float32)
    sorted_cluster = cluster_of[sort_order]
    counts = jnp.zeros((CLUSTERS,), jnp.int32).at[cluster_of].add(1)
    starts = (jnp.cumsum(counts) - counts).astype(jnp.int32)
    capacity = N_GRP * SLOT
    padded = jnp.concatenate([sorted_rows, jnp.zeros((capacity, D), sorted_rows.dtype)], axis=0)
    position = jnp.arange(capacity, dtype=jnp.int32)

    def one_cluster(index):
        window = lax.dynamic_slice(padded, (starts[index].astype(jnp.int32), jnp.int32(0)), (capacity, D))
        live = position < counts[index]
        products = jnp.dot(window, window.T, preferred_element_type=jnp.float32)
        allowed = (position[None, :] < position[:, None]) & live[None, :]
        return lax.optimization_barrier(jnp.max(jnp.where(allowed, products, jnp.float32(-1.0)), axis=1))
    per_cluster = lax.map(one_cluster, jnp.arange(CLUSTERS, dtype=jnp.int32))
    inside = jnp.arange(ROWS_ALL, dtype=jnp.int32) - starts[sorted_cluster]
    sorted_best = per_cluster[sorted_cluster, inside]
    return jnp.zeros((ROWS_ALL,), per_cluster.dtype).at[sort_order].set(sorted_best)
```

```python
import jax
import jax.numpy as jnp
from jax import lax
from jax.experimental import pallas as pl
from jax.experimental.pallas import tpu as pltpu
from jax.sharding import PartitionSpec as P

CLUS_DEV = 2
DIGIT = 128
TAIL = 128


def slots_of(cluster_row, clusters, slot_cap):
    rows = cluster_row.shape[1]
    cluster = lax.broadcasted_iota(jnp.int32, (clusters, rows), 0)
    one_hot = cluster == cluster_row
    before = lax.broadcasted_iota(jnp.int32, (rows, rows), 0) < lax.broadcasted_iota(jnp.int32, (rows, rows), 1)
    running = jnp.dot(
        one_hot.astype(jnp.bfloat16), before.astype(jnp.bfloat16), preferred_element_type=jnp.float32
    )
    within = jnp.sum(jnp.where(one_hot, running, 0.0), axis=0, keepdims=True).astype(jnp.int32)
    return cluster_row * slot_cap + within


def pack_kernel(clusters, slot_cap, rows_ref, cluster_ref, rank_ref, send_ref):
    rows, features = rows_ref.shape
    groups, slots, width = send_ref.shape
    floats = rows_ref[...].astype(jnp.float32)
    unit = (floats * lax.rsqrt(jnp.sum(floats * floats, axis=1, keepdims=True) + 1e-06)).astype(jnp.bfloat16)
    slot_row = slots_of(cluster_ref[...], clusters, slot_cap)
    place = (lax.broadcasted_iota(jnp.int32, (groups * slots, rows), 0) == slot_row).astype(jnp.bfloat16)
    placed = jnp.dot(place, unit, preferred_element_type=jnp.float32)
    send_ref[:, :, :features] = placed.reshape(groups, slots, features).astype(jnp.bfloat16)
    rank_row = rank_ref[...]
    line = lax.broadcasted_iota(jnp.int32, (width - features, rows), 0)
    high = rank_row // DIGIT
    digits = jnp.where(line == 0, high + 1, jnp.where(line == 1, rank_row - high * DIGIT, 0))
    placed_digits = lax.dot_general(
        place,
        digits.astype(jnp.float32).astype(jnp.bfloat16),
        (((1,), (1,)), ((), ())),
        preferred_element_type=jnp.float32,
    )
    send_ref[:, :, features:] = placed_digits.reshape(groups, slots, width - features).astype(jnp.bfloat16)


def score_kernel(slot_cap, features, got_ref, best_ref):
    groups, slots, width = got_ref.shape
    count = groups * slots
    unit = got_ref[:, :, :features].astype(jnp.float32).reshape(count, features).astype(jnp.bfloat16)
    digits = got_ref[:, :, features:].astype(jnp.float32).reshape(count, width - features).astype(jnp.bfloat16)
    lane = lax.broadcasted_iota(jnp.int32, (8, width - features), 1)
    weight = jnp.where(lane == 0, DIGIT, jnp.where(lane == 1, 1, 0)).astype(jnp.float32).astype(jnp.bfloat16)
    dims = (((1,), (1,)), ((), ()))
    rank_row = lax.dot_general(weight, digits, dims, preferred_element_type=jnp.float32)[0:1, :]
    rank_col = lax.dot_general(digits, weight, dims, preferred_element_type=jnp.float32)[:, 0:1]
    products = lax.dot_general(unit, unit, dims, preferred_element_type=jnp.float32)
    cluster_row = lax.broadcasted_iota(jnp.int32, (1, count), 1) % slots // slot_cap
    cluster_col = lax.broadcasted_iota(jnp.int32, (count, 1), 0) % slots // slot_cap
    empty = rank_row < DIGIT
    rank_row = jnp.where(empty, jnp.float32(1e9), rank_row)
    allowed = (rank_row < rank_col) & (cluster_row == cluster_col)
    best = jnp.max(jnp.where(allowed, products, jnp.float32(-1.0)), axis=1, keepdims=True)
    spread = lax.broadcasted_iota(jnp.int32, (count, 128), 1) == lax.broadcasted_iota(jnp.int32, (count, 128), 0) % slots
    lines = jnp.where(spread, best, 0.0).reshape(groups, slots, 128)
    best_ref[...] = jnp.sum(lines, axis=1)


def pick_kernel(clusters, slot_cap, back_ref, cluster_ref, out_ref):
    groups, width = back_ref.shape
    rows = cluster_ref.shape[1]
    slots = CLUS_DEV * slot_cap
    slot_row = slots_of(cluster_ref[...], clusters, slot_cap)
    owner_row = slot_row // slots
    owner = (lax.broadcasted_iota(jnp.int32, (groups, rows), 0) == owner_row).astype(jnp.float32)
    lines = lax.dot_general(
        back_ref[...],
        owner,
        (((0,), (0,)), ((), ())),
        precision=lax.Precision.HIGHEST,
        preferred_element_type=jnp.float32,
    )
    mine = lax.broadcasted_iota(jnp.int32, (width, rows), 0) == slot_row - owner_row * slots
    out_ref[...] = jnp.sum(jnp.where(mine, lines, 0.0), axis=0, keepdims=True)


def local(embeddings, cluster_ids, ranks):
    groups = lax.axis_size("grp")
    rows, features = embeddings.shape
    clusters = CLUS_DEV * groups
    slot_cap = 2 * rows // clusters
    slots = CLUS_DEV * slot_cap
    cluster_row = cluster_ids.reshape(1, rows)
    rank_row = ranks.reshape(1, rows)
    params = pltpu.CompilerParams(vmem_limit_bytes=48 * 1024 * 1024)

    def pack(*refs):
        pack_kernel(clusters, slot_cap, *refs)

    def score(*refs):
        score_kernel(slot_cap, features, *refs)

    def pick(*refs):
        pick_kernel(clusters, slot_cap, *refs)

    send = pl.pallas_call(
        pack,
        out_shape=jax.ShapeDtypeStruct((groups, slots, features + TAIL), jnp.bfloat16),
        compiler_params=params,
        name="pack_rows",
    )(embeddings, cluster_row, rank_row)
    got = lax.all_to_all(send, "grp", split_axis=0, concat_axis=0, tiled=True)
    best = pl.pallas_call(
        score,
        out_shape=jax.ShapeDtypeStruct((groups, 128), jnp.float32),
        compiler_params=params,
        name="score_rows",
    )(got)
    back = lax.all_to_all(best, "grp", split_axis=0, concat_axis=0, tiled=True)
    out = pl.pallas_call(
        pick,
        out_shape=jax.ShapeDtypeStruct((1, rows), jnp.float32),
        compiler_params=params,
        name="pick_rows",
    )(back, cluster_row)
    return out.reshape(rows)


def solution(mesh):
    in_specs = (P(("shard", "grp"), None), P(("shard", "grp"), None), P(("shard", "grp")))
    out_specs = P(("shard", "grp"))
    return jax.shard_map(local, mesh=mesh, in_specs=in_specs, out_specs=out_specs, check_vma=False)
```

```python
import jax
import jax.numpy as jnp
from jax import lax
from jax.experimental import pallas as pl
from jax.experimental.pallas import tpu as pltpu
from jax.sharding import PartitionSpec as P

CLUS_DEV = 2
DIGIT = 128
LANES = 128


def lines_of(slots, features):
    return slots * (features // LANES) + 2


def slots_of(cluster_row, clusters, slot_cap):
    rows = cluster_row.shape[1]
    cluster = lax.broadcasted_iota(jnp.int32, (clusters, rows), 0)
    one_hot = cluster == cluster_row
    before = lax.broadcasted_iota(jnp.int32, (rows, rows), 0) < lax.broadcasted_iota(jnp.int32, (rows, rows), 1)
    running = jnp.dot(
        one_hot.astype(jnp.bfloat16), before.astype(jnp.bfloat16), preferred_element_type=jnp.float32
    )
    within = jnp.sum(jnp.where(one_hot, running, 0.0), axis=0, keepdims=True).astype(jnp.int32)
    return cluster_row * slot_cap + within


def one_hot_bf16(hit):
    return hit.astype(jnp.float32).astype(jnp.bfloat16)


def pack_kernel(clusters, slot_cap, rows_ref, cluster_ref, rank_ref, send_ref, lines_ref):
    rows, features = rows_ref.shape
    slots = CLUS_DEV * slot_cap
    groups = clusters // CLUS_DEV
    span = lines_of(slots, features)
    floats = rows_ref[...].astype(jnp.float32)
    unit = (floats * lax.rsqrt(jnp.sum(floats * floats, axis=1, keepdims=True) + 1e-06)).astype(jnp.bfloat16)
    slot_row = slots_of(cluster_ref[...], clusters, slot_cap)
    place = one_hot_bf16(lax.broadcasted_iota(jnp.int32, (groups * slots, rows), 0) == slot_row)
    placed = jnp.dot(place, unit, preferred_element_type=jnp.float32)
    for group in range(groups):
        for block in range(features // LANES):
            lines_ref[group * span + block * slots : group * span + (block + 1) * slots, :] = placed[
                group * slots : (group + 1) * slots, block * LANES : (block + 1) * LANES
            ]
    rank_row = rank_ref[...]
    high = rank_row // DIGIT
    owner_row = slot_row // slots
    owned = lax.broadcasted_iota(jnp.int32, (groups, rows), 0) == owner_row
    lane = one_hot_bf16(lax.broadcasted_iota(jnp.int32, (LANES, rows), 0) == slot_row - owner_row * slots)
    for line, digit in enumerate((high + 1, rank_row - high * DIGIT)):
        digits = jnp.where(owned, digit, 0).astype(jnp.float32).astype(jnp.bfloat16)
        lines_ref[pl.ds(span - 2 + line, groups, stride=span), :] = lax.dot_general(
            digits, lane, (((1,), (1,)), ((), ())), preferred_element_type=jnp.float32
        )
    send_ref[...] = lines_ref[...].astype(jnp.bfloat16)


def score_kernel(slot_cap, groups, features, got_ref, best_ref, lines_ref):
    slots = CLUS_DEV * slot_cap
    count = groups * slots
    span = lines_of(slots, features)
    lines_ref[...] = got_ref[...].astype(jnp.float32)
    unit = jnp.concatenate(
        [
            jnp.concatenate(
                [
                    lines_ref[group * span + block * slots : group * span + (block + 1) * slots, :]
                    for group in range(groups)
                ],
                axis=0,
            ).astype(jnp.bfloat16)
            for block in range(features // LANES)
        ],
        axis=1,
    )
    high = lines_ref[pl.ds(span - 2, groups, stride=span), :]
    low = lines_ref[pl.ds(span - 1, groups, stride=span), :]
    spread = lax.broadcasted_iota(jnp.int32, (count, LANES), 1) == lax.broadcasted_iota(jnp.int32, (count, LANES), 0) % slots
    rank = (high * DIGIT + low).reshape(groups, 1, LANES)
    rank = jnp.broadcast_to(rank, (groups, slots, LANES)).reshape(count, LANES)
    rank_col = jnp.sum(jnp.where(spread, rank, 0.0), axis=1, keepdims=True)
    lane = lax.broadcasted_iota(jnp.int32, (LANES, count), 0) == lax.broadcasted_iota(jnp.int32, (LANES, count), 1) % slots
    spread_row = jnp.dot(
        high.astype(jnp.bfloat16), one_hot_bf16(lane) * DIGIT, preferred_element_type=jnp.float32
    ) + jnp.dot(low.astype(jnp.bfloat16), one_hot_bf16(lane), preferred_element_type=jnp.float32)
    mine = lax.broadcasted_iota(jnp.int32, (groups, count), 0) == lax.broadcasted_iota(jnp.int32, (groups, count), 1) // slots
    rank_row = jnp.sum(jnp.where(mine, spread_row, 0.0), axis=0, keepdims=True)
    products = lax.dot_general(unit, unit, (((1,), (1,)), ((), ())), preferred_element_type=jnp.float32)
    cluster_row = lax.broadcasted_iota(jnp.int32, (1, count), 1) % slots // slot_cap
    cluster_col = lax.broadcasted_iota(jnp.int32, (count, 1), 0) % slots // slot_cap
    rank_row = jnp.where(rank_row < DIGIT, jnp.float32(1e9), rank_row)
    allowed = (rank_row < rank_col) & (cluster_row == cluster_col)
    best = jnp.max(jnp.where(allowed, products, jnp.float32(-1.0)), axis=1, keepdims=True)
    best_ref[...] = jnp.sum(jnp.where(spread, best, 0.0).reshape(groups, slots, LANES), axis=1)


def pick_kernel(clusters, slot_cap, back_ref, cluster_ref, out_ref):
    groups, width = back_ref.shape
    rows = cluster_ref.shape[1]
    slots = CLUS_DEV * slot_cap
    slot_row = slots_of(cluster_ref[...], clusters, slot_cap)
    owner_row = slot_row // slots
    owner = (lax.broadcasted_iota(jnp.int32, (groups, rows), 0) == owner_row).astype(jnp.float32)
    lines = lax.dot_general(
        back_ref[...],
        owner,
        (((0,), (0,)), ((), ())),
        precision=lax.Precision.HIGHEST,
        preferred_element_type=jnp.float32,
    )
    mine = lax.broadcasted_iota(jnp.int32, (width, rows), 0) == slot_row - owner_row * slots
    out_ref[...] = jnp.sum(jnp.where(mine, lines, 0.0), axis=0, keepdims=True)


def local(embeddings, cluster_ids, ranks):
    groups = lax.axis_size("grp")
    rows, features = embeddings.shape
    clusters = CLUS_DEV * groups
    slot_cap = 2 * rows // clusters
    slots = CLUS_DEV * slot_cap
    cluster_row = cluster_ids.reshape(1, rows)
    rank_row = ranks.reshape(1, rows)
    params = pltpu.CompilerParams(vmem_limit_bytes=48 * 1024 * 1024)

    def pack(*refs):
        pack_kernel(clusters, slot_cap, *refs)

    def score(*refs):
        score_kernel(slot_cap, groups, features, *refs)

    def pick(*refs):
        pick_kernel(clusters, slot_cap, *refs)

    span = lines_of(slots, features)
    lines = pltpu.VMEM((groups * span, LANES), jnp.float32)
    send = pl.pallas_call(
        pack,
        out_shape=jax.ShapeDtypeStruct((groups * span, LANES), jnp.bfloat16),
        scratch_shapes=[lines],
        compiler_params=params,
        name="pack_rows",
    )(embeddings, cluster_row, rank_row)
    got = lax.all_to_all(
        send.reshape(groups, span // 2, 2, LANES), "grp", split_axis=0, concat_axis=0, tiled=True
    ).reshape(groups * span, LANES)
    best = pl.pallas_call(
        score,
        out_shape=jax.ShapeDtypeStruct((groups, LANES), jnp.float32),
        scratch_shapes=[lines],
        compiler_params=params,
        name="score_rows",
    )(got)
    back = lax.all_to_all(best, "grp", split_axis=0, concat_axis=0, tiled=True)
    out = pl.pallas_call(
        pick,
        out_shape=jax.ShapeDtypeStruct((1, rows), jnp.float32),
        compiler_params=params,
        name="pick_rows",
    )(back, cluster_row)
    return out.reshape(rows)


def solution(mesh):
    in_specs = (P(("shard", "grp"), None), P(("shard", "grp"), None), P(("shard", "grp")))
    out_specs = P(("shard", "grp"))
    return jax.shard_map(local, mesh=mesh, in_specs=in_specs, out_specs=out_specs, check_vma=False)
```

```python
import jax
import jax.numpy as jnp
from jax import lax
from jax.experimental import pallas as pl
from jax.experimental.pallas import tpu as pltpu
from jax.sharding import PartitionSpec as P

CLUS_DEV = 2
DIGIT = 128
LANES = 128


def lines_of(slots, features):
    return slots * (features // LANES) + 2


def slots_of(cluster_row, clusters, slot_cap):
    rows = cluster_row.shape[1]
    cluster = lax.broadcasted_iota(jnp.int32, (clusters, rows), 0)
    one_hot = cluster == cluster_row
    before = lax.broadcasted_iota(jnp.int32, (rows, rows), 0) < lax.broadcasted_iota(jnp.int32, (rows, rows), 1)
    running = jnp.dot(
        one_hot.astype(jnp.bfloat16), before.astype(jnp.bfloat16), preferred_element_type=jnp.float32
    )
    within = jnp.sum(jnp.where(one_hot, running, 0.0), axis=0, keepdims=True).astype(jnp.int32)
    return cluster_row * slot_cap + within


def one_hot_bf16(hit):
    return hit.astype(jnp.float32).astype(jnp.bfloat16)


def pack_kernel(
    clusters, slot_cap, rows_hbm, cluster_hbm, rank_hbm, send_ref, slot_ref, rows_ref, cluster_ref, rank_ref, lines_ref, sems
):
    rows, features = rows_ref.shape
    slots = CLUS_DEV * slot_cap
    groups = clusters // CLUS_DEV
    span = lines_of(slots, features)
    copies = [
        pltpu.make_async_copy(source, target, sems.at[index])
        for index, (source, target) in enumerate(
            ((cluster_hbm, cluster_ref), (rank_hbm, rank_ref), (rows_hbm, rows_ref))
        )
    ]
    for copy in copies:
        copy.start()
    copies[0].wait()
    slot_row = slots_of(cluster_ref[...], clusters, slot_cap)
    slot_ref[...] = slot_row
    place = one_hot_bf16(lax.broadcasted_iota(jnp.int32, (groups * slots, rows), 0) == slot_row)
    copies[1].wait()
    rank_row = rank_ref[...]
    high = rank_row // DIGIT
    owner_row = slot_row // slots
    owned = lax.broadcasted_iota(jnp.int32, (groups, rows), 0) == owner_row
    lane = one_hot_bf16(lax.broadcasted_iota(jnp.int32, (LANES, rows), 0) == slot_row - owner_row * slots)
    for line, digit in enumerate((high + 1, rank_row - high * DIGIT)):
        digits = jnp.where(owned, digit, 0).astype(jnp.float32).astype(jnp.bfloat16)
        lines_ref[pl.ds(span - 2 + line, groups, stride=span), :] = lax.dot_general(
            digits, lane, (((1,), (1,)), ((), ())), preferred_element_type=jnp.float32
        )
    copies[2].wait()
    floats = rows_ref[...].astype(jnp.float32)
    unit = (floats * lax.rsqrt(jnp.sum(floats * floats, axis=1, keepdims=True) + 1e-06)).astype(jnp.bfloat16)
    placed = jnp.dot(place, unit, preferred_element_type=jnp.float32)
    for group in range(groups):
        for block in range(features // LANES):
            lines_ref[group * span + block * slots : group * span + (block + 1) * slots, :] = placed[
                group * slots : (group + 1) * slots, block * LANES : (block + 1) * LANES
            ]
    send_ref[...] = lines_ref[...].astype(jnp.bfloat16)


def score_kernel(slot_cap, groups, features, got_ref, best_ref, lines_ref):
    slots = CLUS_DEV * slot_cap
    count = groups * slots
    span = lines_of(slots, features)
    lines_ref[...] = got_ref[...].astype(jnp.float32)
    unit = jnp.concatenate(
        [
            jnp.concatenate(
                [
                    lines_ref[group * span + block * slots : group * span + (block + 1) * slots, :]
                    for group in range(groups)
                ],
                axis=0,
            ).astype(jnp.bfloat16)
            for block in range(features // LANES)
        ],
        axis=1,
    )
    high = lines_ref[pl.ds(span - 2, groups, stride=span), :]
    low = lines_ref[pl.ds(span - 1, groups, stride=span), :]
    spread = lax.broadcasted_iota(jnp.int32, (count, LANES), 1) == lax.broadcasted_iota(jnp.int32, (count, LANES), 0) % slots
    rank = (high * DIGIT + low).reshape(groups, 1, LANES)
    rank = jnp.broadcast_to(rank, (groups, slots, LANES)).reshape(count, LANES)
    rank_col = jnp.sum(jnp.where(spread, rank, 0.0), axis=1, keepdims=True)
    lane = lax.broadcasted_iota(jnp.int32, (LANES, count), 0) == lax.broadcasted_iota(jnp.int32, (LANES, count), 1) % slots
    spread_row = jnp.dot(
        high.astype(jnp.bfloat16), one_hot_bf16(lane) * DIGIT, preferred_element_type=jnp.float32
    ) + jnp.dot(low.astype(jnp.bfloat16), one_hot_bf16(lane), preferred_element_type=jnp.float32)
    mine = lax.broadcasted_iota(jnp.int32, (groups, count), 0) == lax.broadcasted_iota(jnp.int32, (groups, count), 1) // slots
    rank_row = jnp.sum(jnp.where(mine, spread_row, 0.0), axis=0, keepdims=True)
    products = lax.dot_general(unit, unit, (((1,), (1,)), ((), ())), preferred_element_type=jnp.float32)
    cluster_row = lax.broadcasted_iota(jnp.int32, (1, count), 1) % slots // slot_cap
    cluster_col = lax.broadcasted_iota(jnp.int32, (count, 1), 0) % slots // slot_cap
    rank_row = jnp.where(rank_row < DIGIT, jnp.float32(1e9), rank_row)
    allowed = (rank_row < rank_col) & (cluster_row == cluster_col)
    best = jnp.max(jnp.where(allowed, products, jnp.float32(-1.0)), axis=1, keepdims=True)
    best_ref[...] = jnp.sum(jnp.where(spread, best, 0.0).reshape(groups, slots, LANES), axis=1)


def pick_kernel(slots, back_ref, slot_ref, out_ref):
    groups = back_ref.shape[0]
    rows = slot_ref.shape[1]
    ahead = slot_ref[...] - lax.broadcasted_iota(jnp.int32, (groups, rows), 0) * slots
    picked = jnp.zeros((groups, rows), jnp.float32)
    for slot in range(slots):
        picked = jnp.where(ahead == slot, back_ref[:, slot : slot + 1], picked)
    out_ref[...] = jnp.sum(picked, axis=0, keepdims=True)


def local(embeddings, cluster_ids, ranks):
    groups = lax.axis_size("grp")
    rows, features = embeddings.shape
    clusters = CLUS_DEV * groups
    slot_cap = 2 * rows // clusters
    slots = CLUS_DEV * slot_cap
    cluster_row = cluster_ids.reshape(1, rows)
    rank_row = ranks.reshape(1, rows)
    params = pltpu.CompilerParams(vmem_limit_bytes=48 * 1024 * 1024)

    def pack(*refs):
        pack_kernel(clusters, slot_cap, *refs)

    def score(*refs):
        score_kernel(slot_cap, groups, features, *refs)

    def pick(*refs):
        pick_kernel(slots, *refs)

    span = lines_of(slots, features)
    lines = pltpu.VMEM((groups * span, LANES), jnp.float32)
    send, slot_row = pl.pallas_call(
        pack,
        in_specs=[pl.BlockSpec(memory_space=pltpu.HBM)] * 3,
        out_shape=(
            jax.ShapeDtypeStruct((groups * span, LANES), jnp.bfloat16),
            jax.ShapeDtypeStruct((1, rows), jnp.int32),
        ),
        scratch_shapes=[
            pltpu.VMEM((rows, features), jnp.bfloat16),
            pltpu.VMEM((1, rows), jnp.int32),
            pltpu.VMEM((1, rows), jnp.int32),
            lines,
            pltpu.SemaphoreType.DMA((3,)),
        ],
        compiler_params=params,
        name="pack_rows",
    )(*(pltpu.with_memory_space_constraint(x, pltpu.HBM) for x in (embeddings, cluster_row, rank_row)))
    got = lax.all_to_all(
        send.reshape(groups, span // 2, 2, LANES), "grp", split_axis=0, concat_axis=0, tiled=True
    ).reshape(groups * span, LANES)
    best = pl.pallas_call(
        score,
        out_shape=jax.ShapeDtypeStruct((groups, LANES), jnp.float32),
        scratch_shapes=[lines],
        compiler_params=params,
        name="score_rows",
    )(got)
    back = lax.all_to_all(best, "grp", split_axis=0, concat_axis=0, tiled=True)
    out = pl.pallas_call(
        pick,
        out_shape=jax.ShapeDtypeStruct((1, rows), jnp.float32),
        compiler_params=params,
        name="pick_rows",
    )(back, slot_row)
    return out.reshape(rows)


def solution(mesh):
    in_specs = (P(("shard", "grp"), None), P(("shard", "grp"), None), P(("shard", "grp")))
    out_specs = P(("shard", "grp"))
    return jax.shard_map(local, mesh=mesh, in_specs=in_specs, out_specs=out_specs, check_vma=False)
```

```python
import jax
import jax.numpy as jnp
from jax import lax
from jax.experimental import pallas as pl
from jax.experimental.pallas import tpu as pltpu
from jax.sharding import PartitionSpec as P

CLUS_DEV = 2
DIGIT = 128
LANES = 128
FIRST = 38


def lines_of(slots, features):
    return slots * (features // LANES) + 2


def slots_of(cluster_row, clusters, slot_cap):
    rows = cluster_row.shape[1]
    cluster = lax.broadcasted_iota(jnp.int32, (clusters, rows), 0)
    one_hot = cluster == cluster_row
    before = lax.broadcasted_iota(jnp.int32, (rows, rows), 0) < lax.broadcasted_iota(jnp.int32, (rows, rows), 1)
    running = jnp.dot(
        one_hot.astype(jnp.bfloat16), before.astype(jnp.bfloat16), preferred_element_type=jnp.float32
    )
    within = jnp.sum(jnp.where(one_hot, running, 0.0), axis=0, keepdims=True).astype(jnp.int32)
    return cluster_row * slot_cap + within


def one_hot_bf16(hit):
    return hit.astype(jnp.float32).astype(jnp.bfloat16)


def pack_kernel(
    clusters, slot_cap, rows_hbm, cluster_hbm, rank_hbm, send_ref, slot_ref, rows_ref, cluster_ref, rank_ref, lines_ref, sems
):
    rows, features = rows_ref.shape
    slots = CLUS_DEV * slot_cap
    groups = clusters // CLUS_DEV
    span = lines_of(slots, features)
    copies = [
        pltpu.make_async_copy(source, target, sems.at[index])
        for index, (source, target) in enumerate(
            ((cluster_hbm, cluster_ref), (rank_hbm, rank_ref), (rows_hbm, rows_ref))
        )
    ]
    for copy in copies:
        copy.start()
    copies[0].wait()
    slot_row = slots_of(cluster_ref[...], clusters, slot_cap)
    slot_ref[...] = slot_row
    place = one_hot_bf16(lax.broadcasted_iota(jnp.int32, (groups * slots, rows), 0) == slot_row)
    copies[1].wait()
    rank_row = rank_ref[...]
    high = rank_row // DIGIT
    owner_row = slot_row // slots
    owned = lax.broadcasted_iota(jnp.int32, (groups, rows), 0) == owner_row
    lane = one_hot_bf16(lax.broadcasted_iota(jnp.int32, (LANES, rows), 0) == slot_row - owner_row * slots)
    for line, digit in enumerate((high + 1, rank_row - high * DIGIT)):
        digits = jnp.where(owned, digit, 0).astype(jnp.float32).astype(jnp.bfloat16)
        lines_ref[pl.ds(span - 2 + line, groups, stride=span), :] = lax.dot_general(
            digits, lane, (((1,), (1,)), ((), ())), preferred_element_type=jnp.float32
        )
    copies[2].wait()
    floats = rows_ref[...].astype(jnp.float32)
    unit = (floats * lax.rsqrt(jnp.sum(floats * floats, axis=1, keepdims=True) + 1e-06)).astype(jnp.bfloat16)
    placed = jnp.dot(place, unit, preferred_element_type=jnp.float32)
    for group in range(groups):
        for block in range(features // LANES):
            lines_ref[group * span + block * slots : group * span + (block + 1) * slots, :] = placed[
                group * slots : (group + 1) * slots, block * LANES : (block + 1) * LANES
            ]
    send_ref[...] = lines_ref[...].astype(jnp.bfloat16)


def score_kernel(slot_cap, groups, features, got_ref, best_ref, lines_ref):
    slots = CLUS_DEV * slot_cap
    count = groups * slots
    span = lines_of(slots, features)
    lines_ref[...] = got_ref[...].astype(jnp.float32)
    unit = jnp.concatenate(
        [
            jnp.concatenate(
                [
                    lines_ref[group * span + block * slots : group * span + (block + 1) * slots, :]
                    for group in range(groups)
                ],
                axis=0,
            ).astype(jnp.bfloat16)
            for block in range(features // LANES)
        ],
        axis=1,
    )
    high = lines_ref[pl.ds(span - 2, groups, stride=span), :]
    low = lines_ref[pl.ds(span - 1, groups, stride=span), :]
    spread = lax.broadcasted_iota(jnp.int32, (count, LANES), 1) == lax.broadcasted_iota(jnp.int32, (count, LANES), 0) % slots
    rank = (high * DIGIT + low).reshape(groups, 1, LANES)
    rank = jnp.broadcast_to(rank, (groups, slots, LANES)).reshape(count, LANES)
    rank_col = jnp.sum(jnp.where(spread, rank, 0.0), axis=1, keepdims=True)
    lane = lax.broadcasted_iota(jnp.int32, (LANES, count), 0) == lax.broadcasted_iota(jnp.int32, (LANES, count), 1) % slots
    spread_row = jnp.dot(
        high.astype(jnp.bfloat16), one_hot_bf16(lane) * DIGIT, preferred_element_type=jnp.float32
    ) + jnp.dot(low.astype(jnp.bfloat16), one_hot_bf16(lane), preferred_element_type=jnp.float32)
    mine = lax.broadcasted_iota(jnp.int32, (groups, count), 0) == lax.broadcasted_iota(jnp.int32, (groups, count), 1) // slots
    rank_row = jnp.sum(jnp.where(mine, spread_row, 0.0), axis=0, keepdims=True)
    products = lax.dot_general(unit, unit, (((1,), (1,)), ((), ())), preferred_element_type=jnp.float32)
    cluster_row = lax.broadcasted_iota(jnp.int32, (1, count), 1) % slots // slot_cap
    cluster_col = lax.broadcasted_iota(jnp.int32, (count, 1), 0) % slots // slot_cap
    rank_row = jnp.where(rank_row < DIGIT, jnp.float32(1e9), rank_row)
    allowed = (rank_row < rank_col) & (cluster_row == cluster_col)
    best = jnp.max(jnp.where(allowed, products, jnp.float32(-1.0)), axis=1, keepdims=True)
    best_ref[...] = jnp.sum(jnp.where(spread, best, 0.0).reshape(groups, slots, LANES), axis=1)


def pick_kernel(slots, back_ref, slot_ref, out_ref):
    groups = back_ref.shape[0]
    rows = slot_ref.shape[1]
    ahead = slot_ref[...] - lax.broadcasted_iota(jnp.int32, (groups, rows), 0) * slots
    picked = jnp.zeros((groups, rows), jnp.float32)
    for slot in range(slots):
        picked = jnp.where(ahead == slot, back_ref[:, slot : slot + 1], picked)
    out_ref[...] = jnp.sum(picked, axis=0, keepdims=True)


def local(embeddings, cluster_ids, ranks):
    groups = lax.axis_size("grp")
    rows, features = embeddings.shape
    clusters = CLUS_DEV * groups
    slot_cap = 2 * rows // clusters
    slots = CLUS_DEV * slot_cap
    cluster_row = cluster_ids.reshape(1, rows)
    rank_row = ranks.reshape(1, rows)
    params = pltpu.CompilerParams(vmem_limit_bytes=48 * 1024 * 1024)

    def pack(*refs):
        pack_kernel(clusters, slot_cap, *refs)

    def score(*refs):
        score_kernel(slot_cap, groups, features, *refs)

    def pick(*refs):
        pick_kernel(slots, *refs)

    order = [[(FIRST + place) % groups for place in range(groups)]]

    def exchange(pieces):
        return lax.all_to_all(pieces, "grp", split_axis=0, concat_axis=0, axis_index_groups=order, tiled=True)

    span = lines_of(slots, features)
    lines = pltpu.VMEM((groups * span, LANES), jnp.float32)
    send, slot_row = pl.pallas_call(
        pack,
        in_specs=[pl.BlockSpec(memory_space=pltpu.HBM)] * 3,
        out_shape=(
            jax.ShapeDtypeStruct((groups * span, LANES), jnp.bfloat16),
            jax.ShapeDtypeStruct((1, rows), jnp.int32),
        ),
        scratch_shapes=[
            pltpu.VMEM((rows, features), jnp.bfloat16),
            pltpu.VMEM((1, rows), jnp.int32),
            pltpu.VMEM((1, rows), jnp.int32),
            lines,
            pltpu.SemaphoreType.DMA((3,)),
        ],
        compiler_params=params,
        name="pack_rows",
    )(*(pltpu.with_memory_space_constraint(x, pltpu.HBM) for x in (embeddings, cluster_row, rank_row)))
    got = exchange(send.reshape(groups, span // 2, 2, LANES)).reshape(groups * span, LANES)
    best = pl.pallas_call(
        score,
        out_shape=jax.ShapeDtypeStruct((groups, LANES), jnp.float32),
        scratch_shapes=[lines],
        compiler_params=params,
        name="score_rows",
    )(got)
    back = exchange(best)
    out = pl.pallas_call(
        pick,
        out_shape=jax.ShapeDtypeStruct((1, rows), jnp.float32),
        compiler_params=params,
        name="pick_rows",
    )(back, slot_row)
    return out.reshape(rows)


def solution(mesh):
    in_specs = (P(("shard", "grp"), None), P(("shard", "grp"), None), P(("shard", "grp")))
    out_specs = P(("shard", "grp"))
    return jax.shard_map(local, mesh=mesh, in_specs=in_specs, out_specs=out_specs, check_vma=False)
```

```python
import jax
import jax.numpy as jnp
from jax import lax
from jax.experimental import pallas as pl
from jax.experimental.pallas import tpu as pltpu
from jax.sharding import PartitionSpec as P

CLUS_DEV = 2
DIGIT = 128
LANES = 128
FIRST = 38


def lines_of(slots, features):
    return slots * (features // LANES) + 2


def slots_of(cluster_row, clusters, slot_cap):
    rows = cluster_row.shape[1]
    cluster = lax.broadcasted_iota(jnp.int32, (clusters, rows), 0)
    one_hot = cluster == cluster_row
    before = lax.broadcasted_iota(jnp.int32, (rows, rows), 0) < lax.broadcasted_iota(jnp.int32, (rows, rows), 1)
    running = jnp.dot(
        one_hot.astype(jnp.bfloat16), before.astype(jnp.bfloat16), preferred_element_type=jnp.float32
    )
    within = jnp.sum(jnp.where(one_hot, running, 0.0), axis=0, keepdims=True).astype(jnp.int32)
    return cluster_row * slot_cap + within


def one_hot_bf16(hit):
    return hit.astype(jnp.float32).astype(jnp.bfloat16)


def pack_kernel(
    clusters, slot_cap, rows_hbm, cluster_hbm, rank_hbm, send_ref, slot_ref, rows_ref, cluster_ref, rank_ref, lines_ref, sems
):
    rows, features = rows_ref.shape
    slots = CLUS_DEV * slot_cap
    groups = clusters // CLUS_DEV
    span = lines_of(slots, features)
    copies = [
        pltpu.make_async_copy(source, target, sems.at[index])
        for index, (source, target) in enumerate(
            ((cluster_hbm, cluster_ref), (rank_hbm, rank_ref), (rows_hbm, rows_ref))
        )
    ]
    for copy in copies:
        copy.start()
    copies[0].wait()
    slot_row = slots_of(cluster_ref[...], clusters, slot_cap)
    slot_ref[...] = slot_row
    owner_row = slot_row // slots
    inner_row = slot_row - owner_row * slots
    place = one_hot_bf16(
        lax.broadcasted_iota(jnp.int32, (slots * groups, rows), 0) == inner_row * groups + owner_row
    )
    copies[1].wait()
    rank_row = rank_ref[...]
    high = rank_row // DIGIT
    owned = lax.broadcasted_iota(jnp.int32, (groups, rows), 0) == owner_row
    lane = one_hot_bf16(lax.broadcasted_iota(jnp.int32, (LANES, rows), 0) == inner_row)
    for line, digit in enumerate((high + 1, rank_row - high * DIGIT)):
        digits = jnp.where(owned, digit, 0).astype(jnp.float32).astype(jnp.bfloat16)
        lines_ref[pl.ds(span - 2 + line, groups, stride=span), :] = lax.dot_general(
            digits, lane, (((1,), (1,)), ((), ())), preferred_element_type=jnp.float32
        )
    copies[2].wait()
    floats = rows_ref[...].astype(jnp.float32)
    unit = (floats * lax.rsqrt(jnp.sum(floats * floats, axis=1, keepdims=True) + 1e-06)).astype(jnp.bfloat16)
    placed = jnp.dot(place, unit, preferred_element_type=jnp.float32)
    for slot in range(slots):
        for block in range(features // LANES):
            lines_ref[pl.ds(block * slots + slot, groups, stride=span), :] = placed[
                slot * groups : (slot + 1) * groups, block * LANES : (block + 1) * LANES
            ]
    send_ref[...] = lines_ref[...].astype(jnp.bfloat16)


def score_kernel(slot_cap, groups, features, got_ref, best_ref, lines_ref):
    slots = CLUS_DEV * slot_cap
    count = groups * slots
    span = lines_of(slots, features)
    lines_ref[...] = got_ref[...].astype(jnp.float32)
    high = lines_ref[pl.ds(span - 2, groups, stride=span), :] * DIGIT
    low = lines_ref[pl.ds(span - 1, groups, stride=span), :]
    lane = lax.broadcasted_iota(jnp.int32, (groups, LANES), 1)
    ones = jnp.ones((LANES, LANES), jnp.bfloat16)
    dims = (((1,), (1,)), ((), ()))
    best_lines = jnp.zeros((groups, LANES), jnp.float32)
    for cluster in range(CLUS_DEV):
        own_slots = range(cluster * slot_cap, (cluster + 1) * slot_cap)
        unit = jnp.concatenate(
            [
                jnp.concatenate(
                    [lines_ref[pl.ds(block * slots + slot, groups, stride=span), :] for slot in own_slots], axis=0
                ).astype(jnp.bfloat16)
                for block in range(features // LANES)
            ],
            axis=1,
        )
        products = lax.dot_general(unit, unit, dims, preferred_element_type=jnp.float32)
        rank_col = jnp.zeros((slot_cap * groups, LANES), jnp.float32)
        rank_row = jnp.zeros((LANES, slot_cap * groups), jnp.float32)
        for digit in (high, low):
            own = jnp.concatenate([jnp.where(lane == slot, digit, 0.0) for slot in own_slots], axis=0)
            own = own.astype(jnp.bfloat16)
            rank_col += lax.dot_general(own, ones, dims, preferred_element_type=jnp.float32)
            rank_row += lax.dot_general(ones, own, dims, preferred_element_type=jnp.float32)
        rank_row = rank_row[0:1, :]
        rank_row = jnp.where(rank_row < DIGIT, jnp.float32(1e9), rank_row)
        allowed = rank_row < rank_col[:, 0:1]
        best = jnp.max(jnp.where(allowed, products, jnp.float32(-1.0)), axis=1, keepdims=True)
        for place, slot in enumerate(own_slots):
            best_lines = jnp.where(lane == slot, best[place * groups : (place + 1) * groups, :], best_lines)
    best_ref[...] = best_lines


def pick_kernel(slots, back_ref, slot_ref, out_ref):
    groups = back_ref.shape[0]
    rows = slot_ref.shape[1]
    ahead = slot_ref[...] - lax.broadcasted_iota(jnp.int32, (groups, rows), 0) * slots
    picked = jnp.zeros((groups, rows), jnp.float32)
    for slot in range(slots):
        picked = jnp.where(ahead == slot, back_ref[:, slot : slot + 1], picked)
    out_ref[...] = jnp.sum(picked, axis=0, keepdims=True)


def local(embeddings, cluster_ids, ranks):
    groups = lax.axis_size("grp")
    rows, features = embeddings.shape
    clusters = CLUS_DEV * groups
    slot_cap = 2 * rows // clusters
    slots = CLUS_DEV * slot_cap
    cluster_row = cluster_ids.reshape(1, rows)
    rank_row = ranks.reshape(1, rows)
    params = pltpu.CompilerParams(vmem_limit_bytes=48 * 1024 * 1024)

    def pack(*refs):
        pack_kernel(clusters, slot_cap, *refs)

    def score(*refs):
        score_kernel(slot_cap, groups, features, *refs)

    def pick(*refs):
        pick_kernel(slots, *refs)

    order = [[(FIRST + place) % groups for place in range(groups)]]

    def exchange(pieces):
        return lax.all_to_all(pieces, "grp", split_axis=0, concat_axis=0, axis_index_groups=order, tiled=True)

    span = lines_of(slots, features)
    lines = pltpu.VMEM((groups * span, LANES), jnp.float32)
    send, slot_row = pl.pallas_call(
        pack,
        in_specs=[pl.BlockSpec(memory_space=pltpu.HBM)] * 3,
        out_shape=(
            jax.ShapeDtypeStruct((groups * span, LANES), jnp.bfloat16),
            jax.ShapeDtypeStruct((1, rows), jnp.int32),
        ),
        scratch_shapes=[
            pltpu.VMEM((rows, features), jnp.bfloat16),
            pltpu.VMEM((1, rows), jnp.int32),
            pltpu.VMEM((1, rows), jnp.int32),
            lines,
            pltpu.SemaphoreType.DMA((3,)),
        ],
        compiler_params=params,
        name="pack_rows",
    )(*(pltpu.with_memory_space_constraint(x, pltpu.HBM) for x in (embeddings, cluster_row, rank_row)))
    got = exchange(send.reshape(groups, span // 2, 2, LANES)).reshape(groups * span, LANES)
    best = pl.pallas_call(
        score,
        out_shape=jax.ShapeDtypeStruct((groups, LANES), jnp.float32),
        scratch_shapes=[lines],
        compiler_params=params,
        name="score_rows",
    )(got)
    back = exchange(best)
    out = pl.pallas_call(
        pick,
        out_shape=jax.ShapeDtypeStruct((1, rows), jnp.float32),
        compiler_params=params,
        name="pick_rows",
    )(back, slot_row)
    return out.reshape(rows)


def solution(mesh):
    in_specs = (P(("shard", "grp"), None), P(("shard", "grp"), None), P(("shard", "grp")))
    out_specs = P(("shard", "grp"))
    return jax.shard_map(local, mesh=mesh, in_specs=in_specs, out_specs=out_specs, check_vma=False)
```

```python
import jax
import jax.numpy as jnp
from jax import lax
from jax.experimental import pallas as pl
from jax.experimental.pallas import tpu as pltpu
from jax.sharding import PartitionSpec as P

CLUS_DEV = 2
DIGIT = 128
LANES = 128
RINGS = (16, 4)
FIRST = (10, 2)


def order_of_group():
    def distance(place):
        steps = (abs(at - first) for at, first in zip(divmod(place, RINGS[1]), FIRST))
        return sum(min(step, ring - step) for step, ring in zip(steps, RINGS))

    places = range(RINGS[0] * RINGS[1])
    return sorted(places, key=lambda place: (distance(place) > 0, -distance(place), place))


def lines_of(slots, features):
    return slots * (features // LANES) + 2


def slots_of(cluster_row, clusters, slot_cap):
    rows = cluster_row.shape[1]
    cluster = lax.broadcasted_iota(jnp.int32, (clusters, rows), 0)
    one_hot = cluster == cluster_row
    before = lax.broadcasted_iota(jnp.int32, (rows, rows), 0) < lax.broadcasted_iota(jnp.int32, (rows, rows), 1)
    running = jnp.dot(
        one_hot.astype(jnp.bfloat16), before.astype(jnp.bfloat16), preferred_element_type=jnp.float32
    )
    within = jnp.sum(jnp.where(one_hot, running, 0.0), axis=0, keepdims=True).astype(jnp.int32)
    return cluster_row * slot_cap + within


def one_hot_bf16(hit):
    return hit.astype(jnp.float32).astype(jnp.bfloat16)


def pack_kernel(
    clusters, slot_cap, rows_hbm, cluster_hbm, rank_hbm, send_ref, slot_ref, rows_ref, cluster_ref, rank_ref, lines_ref, sems
):
    rows, features = rows_ref.shape
    slots = CLUS_DEV * slot_cap
    groups = clusters // CLUS_DEV
    span = lines_of(slots, features)
    copies = [
        pltpu.make_async_copy(source, target, sems.at[index])
        for index, (source, target) in enumerate(
            ((cluster_hbm, cluster_ref), (rank_hbm, rank_ref), (rows_hbm, rows_ref))
        )
    ]
    for copy in copies:
        copy.start()
    copies[0].wait()
    slot_row = slots_of(cluster_ref[...], clusters, slot_cap)
    slot_ref[...] = slot_row
    owner_row = slot_row // slots
    inner_row = slot_row - owner_row * slots
    place = one_hot_bf16(
        lax.broadcasted_iota(jnp.int32, (slots * groups, rows), 0) == inner_row * groups + owner_row
    )
    copies[1].wait()
    rank_row = rank_ref[...]
    high = rank_row // DIGIT
    owned = lax.broadcasted_iota(jnp.int32, (groups, rows), 0) == owner_row
    lane = one_hot_bf16(lax.broadcasted_iota(jnp.int32, (LANES, rows), 0) == inner_row)
    for line, digit in enumerate((high + 1, rank_row - high * DIGIT)):
        digits = jnp.where(owned, digit, 0).astype(jnp.float32).astype(jnp.bfloat16)
        lines_ref[pl.ds(span - 2 + line, groups, stride=span), :] = lax.dot_general(
            digits, lane, (((1,), (1,)), ((), ())), preferred_element_type=jnp.float32
        )
    copies[2].wait()
    floats = rows_ref[...].astype(jnp.float32)
    unit = (floats * lax.rsqrt(jnp.sum(floats * floats, axis=1, keepdims=True) + 1e-06)).astype(jnp.bfloat16)
    placed = jnp.dot(place, unit, preferred_element_type=jnp.float32)
    for slot in range(slots):
        for block in range(features // LANES):
            lines_ref[pl.ds(block * slots + slot, groups, stride=span), :] = placed[
                slot * groups : (slot + 1) * groups, block * LANES : (block + 1) * LANES
            ]
    send_ref[...] = lines_ref[: groups * span, :].astype(jnp.bfloat16)


def score_kernel(slot_cap, groups, features, got_ref, best_ref, lines_ref):
    slots = CLUS_DEV * slot_cap
    count = groups * slots
    span = lines_of(slots, features)
    lines_ref[: groups * span, :] = got_ref[...].astype(jnp.float32)
    high = lines_ref[pl.ds(span - 2, groups, stride=span), :] * DIGIT
    low = lines_ref[pl.ds(span - 1, groups, stride=span), :]
    lane = lax.broadcasted_iota(jnp.int32, (groups, LANES), 1)
    ones = jnp.ones((LANES, LANES), jnp.bfloat16)
    dims = (((1,), (1,)), ((), ()))
    best_lines = jnp.zeros((groups, LANES), jnp.float32)
    for cluster in range(CLUS_DEV):
        own_slots = range(cluster * slot_cap, (cluster + 1) * slot_cap)
        unit = jnp.concatenate(
            [
                jnp.concatenate(
                    [lines_ref[pl.ds(block * slots + slot, groups, stride=span), :] for slot in own_slots], axis=0
                ).astype(jnp.bfloat16)
                for block in range(features // LANES)
            ],
            axis=1,
        )
        products = lax.dot_general(unit, unit, dims, preferred_element_type=jnp.float32)
        rank_col = jnp.zeros((slot_cap * groups, LANES), jnp.float32)
        rank_row = jnp.zeros((LANES, slot_cap * groups), jnp.float32)
        for digit in (high, low):
            own = jnp.concatenate([jnp.where(lane == slot, digit, 0.0) for slot in own_slots], axis=0)
            own = own.astype(jnp.bfloat16)
            rank_col += lax.dot_general(own, ones, dims, preferred_element_type=jnp.float32)
            rank_row += lax.dot_general(ones, own, dims, preferred_element_type=jnp.float32)
        rank_row = rank_row[0:1, :]
        rank_row = jnp.where(rank_row < DIGIT, jnp.float32(1e9), rank_row)
        allowed = rank_row < rank_col[:, 0:1]
        best = jnp.max(jnp.where(allowed, products, jnp.float32(-1.0)), axis=1, keepdims=True)
        for place, slot in enumerate(own_slots):
            best_lines = jnp.where(lane == slot, best[place * groups : (place + 1) * groups, :], best_lines)
    best_ref[...] = best_lines


def pick_kernel(slots, back_ref, slot_ref, out_ref):
    groups = back_ref.shape[0]
    rows = slot_ref.shape[1]
    ahead = slot_ref[...] - lax.broadcasted_iota(jnp.int32, (groups, rows), 0) * slots
    picked = jnp.zeros((groups, rows), jnp.float32)
    for slot in range(slots):
        picked = jnp.where(ahead == slot, back_ref[:, slot : slot + 1], picked)
    out_ref[...] = jnp.sum(picked, axis=0, keepdims=True)


def local(embeddings, cluster_ids, ranks):
    groups = lax.axis_size("grp")
    rows, features = embeddings.shape
    clusters = CLUS_DEV * groups
    slot_cap = 2 * rows // clusters
    slots = CLUS_DEV * slot_cap
    cluster_row = cluster_ids.reshape(1, rows)
    rank_row = ranks.reshape(1, rows)
    params = pltpu.CompilerParams(vmem_limit_bytes=48 * 1024 * 1024)

    def pack(*refs):
        pack_kernel(clusters, slot_cap, *refs)

    def score(*refs):
        score_kernel(slot_cap, groups, features, *refs)

    def pick(*refs):
        pick_kernel(slots, *refs)

    order = [order_of_group()]

    def exchange(pieces):
        return lax.all_to_all(pieces, "grp", split_axis=0, concat_axis=0, axis_index_groups=order, tiled=True)

    span = lines_of(slots, features)
    lines = pltpu.VMEM((groups * span + 64, LANES), jnp.float32)
    send, slot_row = pl.pallas_call(
        pack,
        in_specs=[pl.BlockSpec(memory_space=pltpu.HBM)] * 3,
        out_shape=(
            jax.ShapeDtypeStruct((groups * span, LANES), jnp.bfloat16),
            jax.ShapeDtypeStruct((1, rows), jnp.int32),
        ),
        scratch_shapes=[
            pltpu.VMEM((rows, features), jnp.bfloat16),
            pltpu.VMEM((1, rows), jnp.int32),
            pltpu.VMEM((1, rows), jnp.int32),
            lines,
            pltpu.SemaphoreType.DMA((3,)),
        ],
        compiler_params=params,
        name="pack_rows",
    )(*(pltpu.with_memory_space_constraint(x, pltpu.HBM) for x in (embeddings, cluster_row, rank_row)))
    got = exchange(send.reshape(groups, span // 2, 2, LANES)).reshape(groups * span, LANES)
    best = pl.pallas_call(
        score,
        out_shape=jax.ShapeDtypeStruct((groups, LANES), jnp.float32),
        scratch_shapes=[lines],
        compiler_params=params,
        name="score_rows",
    )(got)
    back = exchange(best)
    out = pl.pallas_call(
        pick,
        out_shape=jax.ShapeDtypeStruct((1, rows), jnp.float32),
        compiler_params=params,
        name="pick_rows",
    )(back, slot_row)
    return out.reshape(rows)


def solution(mesh):
    in_specs = (P(("shard", "grp"), None), P(("shard", "grp"), None), P(("shard", "grp")))
    out_specs = P(("shard", "grp"))
    return jax.shard_map(local, mesh=mesh, in_specs=in_specs, out_specs=out_specs, check_vma=False)
```

```python
import jax
import jax.numpy as jnp
from jax import lax
from jax.experimental import pallas as pl
from jax.experimental.pallas import tpu as pltpu
from jax.sharding import PartitionSpec as P

CLUS_DEV = 2
DIGIT = 128
LANES = 128
RINGS = (16, 4)
FIRST = (10, 2)


def order_of_group():
    def distance(place):
        steps = (abs(at - first) for at, first in zip(divmod(place, RINGS[1]), FIRST))
        return sum(min(step, ring - step) for step, ring in zip(steps, RINGS))

    places = range(RINGS[0] * RINGS[1])
    return sorted(places, key=lambda place: (distance(place) > 0, -distance(place), place))


def lines_of(slots, features):
    return slots * (features // LANES) + 2


def slots_of(cluster_row, clusters, slot_cap):
    rows = cluster_row.shape[1]
    cluster = lax.broadcasted_iota(jnp.int32, (clusters, rows), 0)
    one_hot = cluster == cluster_row
    before = lax.broadcasted_iota(jnp.int32, (rows, rows), 0) < lax.broadcasted_iota(jnp.int32, (rows, rows), 1)
    running = jnp.dot(
        one_hot.astype(jnp.bfloat16), before.astype(jnp.bfloat16), preferred_element_type=jnp.float32
    )
    within = jnp.sum(jnp.where(one_hot, running, 0.0), axis=0, keepdims=True).astype(jnp.int32)
    return cluster_row * slot_cap + within


def one_hot_bf16(hit):
    return hit.astype(jnp.float32).astype(jnp.bfloat16)


def pack_kernel(
    clusters, slot_cap, rows_hbm, cluster_hbm, rank_hbm, send_ref, slot_ref, rows_ref, cluster_ref, rank_ref, lines_ref, sems
):
    rows, features = rows_ref.shape
    slots = CLUS_DEV * slot_cap
    groups = clusters // CLUS_DEV
    span = lines_of(slots, features)
    copies = [
        pltpu.make_async_copy(source, target, sems.at[index])
        for index, (source, target) in enumerate(
            ((cluster_hbm, cluster_ref), (rank_hbm, rank_ref), (rows_hbm, rows_ref))
        )
    ]
    for copy in copies:
        copy.start()
    copies[0].wait()
    slot_row = slots_of(cluster_ref[...], clusters, slot_cap)
    slot_ref[...] = slot_row
    owner_row = slot_row // slots
    inner_row = slot_row - owner_row * slots
    place = one_hot_bf16(
        lax.broadcasted_iota(jnp.int32, (slots * groups, rows), 0) == inner_row * groups + owner_row
    )
    copies[1].wait()
    rank_row = rank_ref[...]
    high = rank_row // DIGIT
    owned = lax.broadcasted_iota(jnp.int32, (groups, rows), 0) == owner_row
    lane = one_hot_bf16(lax.broadcasted_iota(jnp.int32, (LANES, rows), 0) == inner_row)
    for line, digit in enumerate((high + 1, rank_row - high * DIGIT)):
        digits = jnp.where(owned, digit, 0).astype(jnp.float32).astype(jnp.bfloat16)
        lines_ref[pl.ds(span - 2 + line, groups, stride=span), :] = lax.dot_general(
            digits, lane, (((1,), (1,)), ((), ())), preferred_element_type=jnp.float32
        )
    copies[2].wait()
    floats = rows_ref[...].astype(jnp.float32)
    unit = (floats * lax.rsqrt(jnp.sum(floats * floats, axis=1, keepdims=True) + 1e-06)).astype(jnp.bfloat16)
    placed = jnp.dot(place, unit, preferred_element_type=jnp.float32)
    for slot in range(slots):
        for block in range(features // LANES):
            lines_ref[pl.ds(block * slots + slot, groups, stride=span), :] = placed[
                slot * groups : (slot + 1) * groups, block * LANES : (block + 1) * LANES
            ]
    send_ref[...] = lines_ref[: groups * span, :].astype(jnp.bfloat16)


def score_kernel(slot_cap, groups, features, got_ref, best_ref, lines_ref):
    slots = CLUS_DEV * slot_cap
    count = groups * slots
    span = lines_of(slots, features)
    lines_ref[: groups * span, :] = got_ref[...].astype(jnp.float32)
    high = lines_ref[pl.ds(span - 2, groups, stride=span), :] * DIGIT
    low = lines_ref[pl.ds(span - 1, groups, stride=span), :]
    lane = lax.broadcasted_iota(jnp.int32, (groups, LANES), 1)
    ones = jnp.ones((8, LANES), jnp.bfloat16)
    dims = (((1,), (1,)), ((), ()))
    best_lines = jnp.zeros((groups, LANES), jnp.float32)
    for cluster in range(CLUS_DEV):
        own_slots = range(cluster * slot_cap, (cluster + 1) * slot_cap)
        unit = jnp.concatenate(
            [
                jnp.concatenate(
                    [lines_ref[pl.ds(block * slots + slot, groups, stride=span), :] for slot in own_slots], axis=0
                ).astype(jnp.bfloat16)
                for block in range(features // LANES)
            ],
            axis=1,
        )
        products = lax.dot_general(unit, unit, dims, preferred_element_type=jnp.float32)
        rank_col = jnp.zeros((slot_cap * groups, 1), jnp.float32)
        rank_row = jnp.zeros((8, slot_cap * groups), jnp.float32)
        for digit in (high, low):
            own = jnp.concatenate([jnp.where(lane == slot, digit, 0.0) for slot in own_slots], axis=0)
            own = own.astype(jnp.bfloat16)
            rank_col += jnp.sum(own.astype(jnp.float32), axis=1, keepdims=True)
            rank_row += lax.dot_general(ones, own, dims, preferred_element_type=jnp.float32)
        rank_row = rank_row[0:1, :]
        rank_row = jnp.where(rank_row < DIGIT, jnp.float32(1e9), rank_row)
        allowed = rank_row < rank_col
        best = jnp.max(jnp.where(allowed, products, jnp.float32(-1.0)), axis=1, keepdims=True)
        for place, slot in enumerate(own_slots):
            best_lines = jnp.where(lane == slot, best[place * groups : (place + 1) * groups, :], best_lines)
    best_ref[...] = best_lines


def pick_kernel(slots, back_ref, slot_ref, out_ref):
    groups = back_ref.shape[0]
    rows = slot_ref.shape[1]
    ahead = slot_ref[...] - lax.broadcasted_iota(jnp.int32, (groups, rows), 0) * slots
    picked = jnp.zeros((groups, rows), jnp.float32)
    for slot in range(slots):
        picked = jnp.where(ahead == slot, back_ref[:, slot : slot + 1], picked)
    out_ref[...] = jnp.sum(picked, axis=0, keepdims=True)


def local(embeddings, cluster_ids, ranks):
    groups = lax.axis_size("grp")
    rows, features = embeddings.shape
    clusters = CLUS_DEV * groups
    slot_cap = 2 * rows // clusters
    slots = CLUS_DEV * slot_cap
    cluster_row = cluster_ids.reshape(1, rows)
    rank_row = ranks.reshape(1, rows)
    params = pltpu.CompilerParams(vmem_limit_bytes=48 * 1024 * 1024)

    def pack(*refs):
        pack_kernel(clusters, slot_cap, *refs)

    def score(*refs):
        score_kernel(slot_cap, groups, features, *refs)

    def pick(*refs):
        pick_kernel(slots, *refs)

    order = [order_of_group()]

    def exchange(pieces):
        return lax.all_to_all(pieces, "grp", split_axis=0, concat_axis=0, axis_index_groups=order, tiled=True)

    span = lines_of(slots, features)
    lines = pltpu.VMEM((groups * span + 64, LANES), jnp.float32)
    send, slot_row = pl.pallas_call(
        pack,
        in_specs=[pl.BlockSpec(memory_space=pltpu.HBM)] * 3,
        out_shape=(
            jax.ShapeDtypeStruct((groups * span, LANES), jnp.bfloat16),
            jax.ShapeDtypeStruct((1, rows), jnp.int32),
        ),
        scratch_shapes=[
            pltpu.VMEM((rows, features), jnp.bfloat16),
            pltpu.VMEM((1, rows), jnp.int32),
            pltpu.VMEM((1, rows), jnp.int32),
            lines,
            pltpu.SemaphoreType.DMA((3,)),
        ],
        compiler_params=params,
        name="pack_rows",
    )(*(pltpu.with_memory_space_constraint(x, pltpu.HBM) for x in (embeddings, cluster_row, rank_row)))
    got = exchange(send.reshape(groups, span // 2, 2, LANES)).reshape(groups * span, LANES)
    best = pl.pallas_call(
        score,
        out_shape=jax.ShapeDtypeStruct((groups, LANES), jnp.float32),
        scratch_shapes=[lines],
        compiler_params=params,
        name="score_rows",
    )(got)
    back = exchange(best)
    out = pl.pallas_call(
        pick,
        out_shape=jax.ShapeDtypeStruct((1, rows), jnp.float32),
        compiler_params=params,
        name="pick_rows",
    )(back, slot_row)
    return out.reshape(rows)


def solution(mesh):
    in_specs = (P(("shard", "grp"), None), P(("shard", "grp"), None), P(("shard", "grp")))
    out_specs = P(("shard", "grp"))
    return jax.shard_map(local, mesh=mesh, in_specs=in_specs, out_specs=out_specs, check_vma=False)
```

```python
import jax
import jax.numpy as jnp
from jax import lax
from jax.experimental import pallas as pl
from jax.experimental.pallas import tpu as pltpu
from jax.sharding import PartitionSpec as P

CLUS_DEV = 2
DIGIT = 128
LANES = 128
RINGS = (16, 4)
FIRST = (10, 2)


def order_of_group():
    def distance(place):
        steps = (abs(at - first) for at, first in zip(divmod(place, RINGS[1]), FIRST))
        return sum(min(step, ring - step) for step, ring in zip(steps, RINGS))

    places = range(RINGS[0] * RINGS[1])
    return sorted(places, key=lambda place: (distance(place) > 0, -distance(place), place))


def lines_of(slots, features):
    return slots * (features // LANES) + 2


def slots_of(cluster_row, clusters, slot_cap):
    rows = cluster_row.shape[1]
    cluster = lax.broadcasted_iota(jnp.int32, (clusters, rows), 0)
    one_hot = cluster == cluster_row
    before = lax.broadcasted_iota(jnp.int32, (rows, rows), 0) < lax.broadcasted_iota(jnp.int32, (rows, rows), 1)
    running = jnp.dot(
        one_hot.astype(jnp.bfloat16), before.astype(jnp.bfloat16), preferred_element_type=jnp.float32
    )
    within = jnp.sum(jnp.where(one_hot, running, 0.0), axis=0, keepdims=True).astype(jnp.int32)
    return cluster_row * slot_cap + within


def one_hot_bf16(hit):
    return hit.astype(jnp.float32).astype(jnp.bfloat16)


def pack_kernel(
    clusters, slot_cap, rows_hbm, cluster_hbm, rank_hbm, send_ref, slot_ref, rows_ref, cluster_ref, rank_ref, lines_ref, sems
):
    rows, features = rows_ref.shape
    slots = CLUS_DEV * slot_cap
    groups = clusters // CLUS_DEV
    span = lines_of(slots, features)
    copies = [
        pltpu.make_async_copy(source, target, sems.at[index])
        for index, (source, target) in enumerate(
            ((cluster_hbm, cluster_ref), (rank_hbm, rank_ref), (rows_hbm, rows_ref))
        )
    ]
    for copy in copies:
        copy.start()
    copies[0].wait()
    slot_row = slots_of(cluster_ref[...], clusters, slot_cap)
    slot_ref[...] = slot_row
    owner_row = slot_row // slots
    inner_row = slot_row - owner_row * slots
    place = one_hot_bf16(
        lax.broadcasted_iota(jnp.int32, (slots * groups, rows), 0) == inner_row * groups + owner_row
    )
    copies[1].wait()
    rank_row = rank_ref[...]
    high = rank_row // DIGIT
    owned = lax.broadcasted_iota(jnp.int32, (groups, rows), 0) == owner_row
    lane = one_hot_bf16(lax.broadcasted_iota(jnp.int32, (LANES, rows), 0) == inner_row)
    for line, digit in enumerate((high + 1, rank_row - high * DIGIT)):
        digits = jnp.where(owned, digit, 0).astype(jnp.float32).astype(jnp.bfloat16)
        lines_ref[pl.ds(span - 2 + line, groups, stride=span), :] = lax.dot_general(
            digits, lane, (((1,), (1,)), ((), ())), preferred_element_type=jnp.float32
        )
    copies[2].wait()
    floats = rows_ref[...].astype(jnp.float32)
    unit = (floats * lax.rsqrt(jnp.sum(floats * floats, axis=1, keepdims=True) + 1e-06)).astype(jnp.bfloat16)
    placed = jnp.dot(place, unit, preferred_element_type=jnp.float32)
    for slot in range(slots):
        for block in range(features // LANES):
            lines_ref[pl.ds(block * slots + slot, groups, stride=span), :] = placed[
                slot * groups : (slot + 1) * groups, block * LANES : (block + 1) * LANES
            ]
    send_ref[...] = lines_ref[: groups * span, :].astype(jnp.bfloat16)


def score_kernel(slot_cap, groups, features, got_ref, best_ref, lines_ref):
    slots = CLUS_DEV * slot_cap
    count = groups * slots
    span = lines_of(slots, features)
    lines_ref[: groups * span, :] = got_ref[...].astype(jnp.float32)
    high = lines_ref[pl.ds(span - 2, groups, stride=span), :] * DIGIT
    low = lines_ref[pl.ds(span - 1, groups, stride=span), :]
    lane = lax.broadcasted_iota(jnp.int32, (groups, LANES), 1)
    ones = jnp.ones((8, LANES), jnp.bfloat16)
    dims = (((1,), (1,)), ((), ()))
    best_lines = jnp.zeros((groups, LANES), jnp.float32)
    for cluster in range(CLUS_DEV):
        own_slots = range(cluster * slot_cap, (cluster + 1) * slot_cap)
        unit = jnp.concatenate(
            [
                jnp.concatenate(
                    [lines_ref[pl.ds(block * slots + slot, groups, stride=span), :] for slot in own_slots], axis=0
                ).astype(jnp.bfloat16)
                for block in range(features // LANES)
            ],
            axis=1,
        )
        products = lax.dot_general(unit, unit, dims, preferred_element_type=jnp.float32)
        rank_col = jnp.zeros((slot_cap * groups, 1), jnp.float32)
        rank_row = jnp.zeros((8, slot_cap * groups), jnp.float32)
        for digit in (high, low):
            own = jnp.concatenate([jnp.where(lane == slot, digit, 0.0) for slot in own_slots], axis=0)
            own = own.astype(jnp.bfloat16)
            rank_col += jnp.sum(own.astype(jnp.float32), axis=1, keepdims=True)
            rank_row += lax.dot_general(ones, own, dims, preferred_element_type=jnp.float32)
        rank_row = rank_row[0:1, :]
        rank_row = jnp.where(rank_row < DIGIT, jnp.float32(1e9), rank_row)
        allowed = rank_row < rank_col
        best = jnp.max(jnp.where(allowed, products, jnp.float32(-1.0)), axis=1, keepdims=True)
        for place, slot in enumerate(own_slots):
            best_lines = jnp.where(lane == slot, best[place * groups : (place + 1) * groups, :], best_lines)
    best_ref[...] = best_lines


def pick_kernel(slots, back_ref, slot_ref, out_ref):
    groups = back_ref.shape[0]
    rows = slot_ref.shape[1]
    ahead = slot_ref[...] - lax.broadcasted_iota(jnp.int32, (groups, rows), 0) * slots
    picked = jnp.zeros((groups, rows), jnp.float32)
    for slot in range(slots):
        picked = jnp.where(ahead == slot, back_ref[:, slot : slot + 1], picked)
    out_ref[...] = jnp.sum(picked, axis=0, keepdims=True)


def local(embeddings, cluster_ids, ranks):
    groups = lax.axis_size("grp")
    rows, features = embeddings.shape
    clusters = CLUS_DEV * groups
    slot_cap = 2 * rows // clusters
    slots = CLUS_DEV * slot_cap
    cluster_row = cluster_ids.reshape(1, rows)
    rank_row = ranks.reshape(1, rows)
    params = pltpu.CompilerParams(vmem_limit_bytes=48 * 1024 * 1024)

    def pack(*refs):
        pack_kernel(clusters, slot_cap, *refs)

    def score(*refs):
        score_kernel(slot_cap, groups, features, *refs)

    def pick(*refs):
        pick_kernel(slots, *refs)

    first, *others = order_of_group()
    half = len(others) // 2
    turned = [first] + others[half:] + others[:half]
    order = [
        [shard * groups + place for place in (turned if shard % 2 else [first] + others)]
        for shard in range(lax.axis_size("shard"))
    ]

    def exchange(pieces):
        return lax.all_to_all(
            pieces, ("shard", "grp"), split_axis=0, concat_axis=0, axis_index_groups=order, tiled=True
        )

    span = lines_of(slots, features)
    lines = pltpu.VMEM((groups * span + 64, LANES), jnp.float32)
    send, slot_row = pl.pallas_call(
        pack,
        in_specs=[pl.BlockSpec(memory_space=pltpu.HBM)] * 3,
        out_shape=(
            jax.ShapeDtypeStruct((groups * span, LANES), jnp.bfloat16),
            jax.ShapeDtypeStruct((1, rows), jnp.int32),
        ),
        scratch_shapes=[
            pltpu.VMEM((rows, features), jnp.bfloat16),
            pltpu.VMEM((1, rows), jnp.int32),
            pltpu.VMEM((1, rows), jnp.int32),
            lines,
            pltpu.SemaphoreType.DMA((3,)),
        ],
        compiler_params=params,
        name="pack_rows",
    )(*(pltpu.with_memory_space_constraint(x, pltpu.HBM) for x in (embeddings, cluster_row, rank_row)))
    got = exchange(send.reshape(groups, span // 2, 2, LANES)).reshape(groups * span, LANES)
    best = pl.pallas_call(
        score,
        out_shape=jax.ShapeDtypeStruct((groups, LANES), jnp.float32),
        scratch_shapes=[lines],
        compiler_params=params,
        name="score_rows",
    )(got)
    back = exchange(best)
    out = pl.pallas_call(
        pick,
        out_shape=jax.ShapeDtypeStruct((1, rows), jnp.float32),
        compiler_params=params,
        name="pick_rows",
    )(back, slot_row)
    return out.reshape(rows)


def solution(mesh):
    in_specs = (P(("shard", "grp"), None), P(("shard", "grp"), None), P(("shard", "grp")))
    out_specs = P(("shard", "grp"))
    return jax.shard_map(local, mesh=mesh, in_specs=in_specs, out_specs=out_specs, check_vma=False)
```

```python
import jax
import jax.numpy as jnp
from jax import lax
from jax.experimental import pallas as pl
from jax.experimental.pallas import tpu as pltpu
from jax.sharding import PartitionSpec as P

CLUS_DEV = 2
DIGIT = 128
LANES = 128
RINGS = (16, 4)
FIRST = (10, 2)


def order_of_group():
    def distance(place):
        steps = (abs(at - first) for at, first in zip(divmod(place, RINGS[1]), FIRST))
        return sum(min(step, ring - step) for step, ring in zip(steps, RINGS))

    places = range(RINGS[0] * RINGS[1])
    return sorted(places, key=lambda place: (distance(place) > 0, -distance(place), place))


def lines_of(slots, features):
    return slots * (features // LANES) + 2


def slots_of(cluster_row, clusters, slot_cap):
    rows = cluster_row.shape[1]
    cluster = lax.broadcasted_iota(jnp.int32, (clusters, rows), 0)
    one_hot = cluster == cluster_row
    before = lax.broadcasted_iota(jnp.int32, (rows, rows), 0) < lax.broadcasted_iota(jnp.int32, (rows, rows), 1)
    running = jnp.dot(
        one_hot.astype(jnp.bfloat16), before.astype(jnp.bfloat16), preferred_element_type=jnp.float32
    )
    within = jnp.sum(jnp.where(one_hot, running, 0.0), axis=0, keepdims=True).astype(jnp.int32)
    return cluster_row * slot_cap + within


def one_hot_bf16(hit):
    return hit.astype(jnp.float32).astype(jnp.bfloat16)


def pack_kernel(
    clusters, slot_cap, rows_hbm, cluster_hbm, rank_hbm, send_ref, slot_ref, rows_ref, cluster_ref, rank_ref, lines_ref, sems
):
    rows, features = rows_ref.shape
    slots = CLUS_DEV * slot_cap
    groups = clusters // CLUS_DEV
    span = lines_of(slots, features)
    copies = [
        pltpu.make_async_copy(source, target, sems.at[index])
        for index, (source, target) in enumerate(
            ((cluster_hbm, cluster_ref), (rank_hbm, rank_ref), (rows_hbm, rows_ref))
        )
    ]
    for copy in copies:
        copy.start()
    copies[1].wait()
    copies[0].wait()
    slot_row = slots_of(cluster_ref[...], clusters, slot_cap)
    slot_ref[...] = slot_row
    owner_row = slot_row // slots
    inner_row = slot_row - owner_row * slots
    place = one_hot_bf16(
        lax.broadcasted_iota(jnp.int32, (slots * groups, rows), 0) == inner_row * groups + owner_row
    )
    rank_row = rank_ref[...]
    high = rank_row // DIGIT
    owned = lax.broadcasted_iota(jnp.int32, (groups, rows), 0) == owner_row
    lane = one_hot_bf16(lax.broadcasted_iota(jnp.int32, (LANES, rows), 0) == inner_row)
    for line, digit in enumerate((high + 1, rank_row - high * DIGIT)):
        digits = jnp.where(owned, digit, 0).astype(jnp.float32).astype(jnp.bfloat16)
        lines_ref[pl.ds(span - 2 + line, groups, stride=span), :] = lax.dot_general(
            digits, lane, (((1,), (1,)), ((), ())), preferred_element_type=jnp.float32
        )
    copies[2].wait()
    floats = rows_ref[...].astype(jnp.float32)
    unit = (floats * lax.rsqrt(jnp.sum(floats * floats, axis=1, keepdims=True) + 1e-06)).astype(jnp.bfloat16)
    placed = jnp.dot(place, unit, preferred_element_type=jnp.float32)
    for slot in range(slots):
        for block in range(features // LANES):
            lines_ref[pl.ds(block * slots + slot, groups, stride=span), :] = placed[
                slot * groups : (slot + 1) * groups, block * LANES : (block + 1) * LANES
            ]
    send_ref[...] = lines_ref[: groups * span, :].astype(jnp.bfloat16)


def score_kernel(slot_cap, groups, features, got_ref, best_ref, lines_ref):
    slots = CLUS_DEV * slot_cap
    count = groups * slots
    span = lines_of(slots, features)
    lines_ref[: groups * span, :] = got_ref[...].astype(jnp.float32)
    high = lines_ref[pl.ds(span - 2, groups, stride=span), :] * DIGIT
    low = lines_ref[pl.ds(span - 1, groups, stride=span), :]
    lane = lax.broadcasted_iota(jnp.int32, (groups, LANES), 1)
    ones = jnp.ones((8, LANES), jnp.bfloat16)
    dims = (((1,), (1,)), ((), ()))
    best_lines = jnp.zeros((groups, LANES), jnp.float32)
    for cluster in range(CLUS_DEV):
        own_slots = range(cluster * slot_cap, (cluster + 1) * slot_cap)
        unit = jnp.concatenate(
            [
                jnp.concatenate(
                    [lines_ref[pl.ds(block * slots + slot, groups, stride=span), :] for slot in own_slots], axis=0
                ).astype(jnp.bfloat16)
                for block in range(features // LANES)
            ],
            axis=1,
        )
        products = lax.dot_general(unit, unit, dims, preferred_element_type=jnp.float32)
        rank_col = jnp.zeros((slot_cap * groups, 1), jnp.float32)
        rank_row = jnp.zeros((8, slot_cap * groups), jnp.float32)
        for digit in (high, low):
            own = jnp.concatenate([jnp.where(lane == slot, digit, 0.0) for slot in own_slots], axis=0)
            own = own.astype(jnp.bfloat16)
            rank_col += jnp.sum(own.astype(jnp.float32), axis=1, keepdims=True)
            rank_row += lax.dot_general(ones, own, dims, preferred_element_type=jnp.float32)
        rank_row = rank_row[0:1, :]
        rank_row = jnp.where(rank_row < DIGIT, jnp.float32(1e9), rank_row)
        allowed = rank_row < rank_col
        best = jnp.max(jnp.where(allowed, products, jnp.float32(-1.0)), axis=1, keepdims=True)
        for place, slot in enumerate(own_slots):
            best_lines = jnp.where(lane == slot, best[place * groups : (place + 1) * groups, :], best_lines)
    best_ref[...] = best_lines


def pick_kernel(slots, back_ref, slot_ref, out_ref):
    groups = back_ref.shape[0]
    rows = slot_ref.shape[1]
    ahead = slot_ref[...] - lax.broadcasted_iota(jnp.int32, (groups, rows), 0) * slots
    picked = jnp.zeros((groups, rows), jnp.float32)
    for slot in range(slots):
        picked = jnp.where(ahead == slot, back_ref[:, slot : slot + 1], picked)
    out_ref[...] = jnp.sum(picked, axis=0, keepdims=True)


def local(embeddings, cluster_ids, ranks):
    groups = lax.axis_size("grp")
    rows, features = embeddings.shape
    clusters = CLUS_DEV * groups
    slot_cap = 2 * rows // clusters
    slots = CLUS_DEV * slot_cap
    cluster_row = cluster_ids.reshape(1, rows)
    rank_row = ranks.reshape(1, rows)
    params = pltpu.CompilerParams(vmem_limit_bytes=48 * 1024 * 1024)

    def pack(*refs):
        pack_kernel(clusters, slot_cap, *refs)

    def score(*refs):
        score_kernel(slot_cap, groups, features, *refs)

    def pick(*refs):
        pick_kernel(slots, *refs)

    order = [order_of_group()]

    def exchange(pieces):
        return lax.all_to_all(pieces, "grp", split_axis=0, concat_axis=0, axis_index_groups=order, tiled=True)

    span = lines_of(slots, features)
    lines = pltpu.VMEM((groups * span + 64, LANES), jnp.float32)
    send, slot_row = pl.pallas_call(
        pack,
        in_specs=[pl.BlockSpec(memory_space=pltpu.HBM)] * 3,
        out_shape=(
            jax.ShapeDtypeStruct((groups * span, LANES), jnp.bfloat16),
            jax.ShapeDtypeStruct((1, rows), jnp.int32),
        ),
        scratch_shapes=[
            pltpu.VMEM((rows, features), jnp.bfloat16),
            pltpu.VMEM((1, rows), jnp.int32),
            pltpu.VMEM((1, rows), jnp.int32),
            lines,
            pltpu.SemaphoreType.DMA((3,)),
        ],
        compiler_params=params,
        name="pack_rows",
    )(*(pltpu.with_memory_space_constraint(x, pltpu.HBM) for x in (embeddings, cluster_row, rank_row)))
    got = exchange(send.reshape(groups, span // 2, 2, LANES)).reshape(groups * span, LANES)
    best = pl.pallas_call(
        score,
        out_shape=jax.ShapeDtypeStruct((groups, LANES), jnp.float32),
        scratch_shapes=[lines],
        compiler_params=params,
        name="score_rows",
    )(got)
    back = exchange(best)
    out = pl.pallas_call(
        pick,
        out_shape=jax.ShapeDtypeStruct((1, rows), jnp.float32),
        compiler_params=params,
        name="pick_rows",
    )(back, slot_row)
    return out.reshape(rows)


def solution(mesh):
    in_specs = (P(("shard", "grp"), None), P(("shard", "grp"), None), P(("shard", "grp")))
    out_specs = P(("shard", "grp"))
    return jax.shard_map(local, mesh=mesh, in_specs=in_specs, out_specs=out_specs, check_vma=False)
```

```python
import jax
import jax.numpy as jnp
from jax import lax
from jax.experimental import pallas as pl
from jax.experimental.pallas import tpu as pltpu
from jax.sharding import PartitionSpec as P

CLUS_DEV = 2
DIGIT = 128
LANES = 128
RINGS = (16, 4)
FIRST = (10, 2)


def order_of_group(turn):
    def distance(place):
        steps = (abs(at - first) for at, first in zip(divmod(place, RINGS[1]), FIRST))
        return sum(min(step, ring - step) for step, ring in zip(steps, RINGS))

    places = range(RINGS[0] * RINGS[1])
    return sorted(places, key=lambda place: (distance(place) > 0, -distance(place), turn * place))


def lines_of(slots, features):
    return slots * (features // LANES) + 2


def slots_of(cluster_row, clusters, slot_cap):
    rows = cluster_row.shape[1]
    cluster = lax.broadcasted_iota(jnp.int32, (clusters, rows), 0)
    one_hot = cluster == cluster_row
    before = lax.broadcasted_iota(jnp.int32, (rows, rows), 0) < lax.broadcasted_iota(jnp.int32, (rows, rows), 1)
    running = jnp.dot(
        one_hot.astype(jnp.bfloat16), before.astype(jnp.bfloat16), preferred_element_type=jnp.float32
    )
    within = jnp.sum(jnp.where(one_hot, running, 0.0), axis=0, keepdims=True).astype(jnp.int32)
    return cluster_row * slot_cap + within


def one_hot_bf16(hit):
    return hit.astype(jnp.float32).astype(jnp.bfloat16)


def pack_kernel(
    clusters, slot_cap, rows_hbm, cluster_hbm, rank_hbm, send_ref, slot_ref, rows_ref, cluster_ref, rank_ref, lines_ref, sems
):
    rows, features = rows_ref.shape
    slots = CLUS_DEV * slot_cap
    groups = clusters // CLUS_DEV
    span = lines_of(slots, features)
    copies = [
        pltpu.make_async_copy(source, target, sems.at[index])
        for index, (source, target) in enumerate(
            ((cluster_hbm, cluster_ref), (rank_hbm, rank_ref), (rows_hbm, rows_ref))
        )
    ]
    for copy in copies:
        copy.start()
    copies[0].wait()
    slot_row = slots_of(cluster_ref[...], clusters, slot_cap)
    slot_ref[...] = slot_row
    owner_row = slot_row // slots
    inner_row = slot_row - owner_row * slots
    place = one_hot_bf16(
        lax.broadcasted_iota(jnp.int32, (slots * groups, rows), 0) == inner_row * groups + owner_row
    )
    copies[1].wait()
    rank_row = rank_ref[...]
    high = rank_row // DIGIT
    owned = lax.broadcasted_iota(jnp.int32, (groups, rows), 0) == owner_row
    lane = one_hot_bf16(lax.broadcasted_iota(jnp.int32, (LANES, rows), 0) == inner_row)
    for line, digit in enumerate((high + 1, rank_row - high * DIGIT)):
        digits = jnp.where(owned, digit, 0).astype(jnp.float32).astype(jnp.bfloat16)
        lines_ref[pl.ds(span - 2 + line, groups, stride=span), :] = lax.dot_general(
            digits, lane, (((1,), (1,)), ((), ())), preferred_element_type=jnp.float32
        )
    copies[2].wait()
    floats = rows_ref[...].astype(jnp.float32)
    unit = (floats * lax.rsqrt(jnp.sum(floats * floats, axis=1, keepdims=True) + 1e-06)).astype(jnp.bfloat16)
    placed = jnp.dot(place, unit, preferred_element_type=jnp.float32)
    for slot in range(slots):
        for block in range(features // LANES):
            lines_ref[pl.ds(block * slots + slot, groups, stride=span), :] = placed[
                slot * groups : (slot + 1) * groups, block * LANES : (block + 1) * LANES
            ]
    send_ref[...] = lines_ref[: groups * span, :].astype(jnp.bfloat16)


def score_kernel(slot_cap, groups, features, got_ref, best_ref, lines_ref):
    slots = CLUS_DEV * slot_cap
    count = groups * slots
    span = lines_of(slots, features)
    lines_ref[: groups * span, :] = got_ref[...].astype(jnp.float32)
    high = lines_ref[pl.ds(span - 2, groups, stride=span), :] * DIGIT
    low = lines_ref[pl.ds(span - 1, groups, stride=span), :]
    lane = lax.broadcasted_iota(jnp.int32, (groups, LANES), 1)
    ones = jnp.ones((8, LANES), jnp.bfloat16)
    dims = (((1,), (1,)), ((), ()))
    best_lines = jnp.zeros((groups, LANES), jnp.float32)
    for cluster in range(CLUS_DEV):
        own_slots = range(cluster * slot_cap, (cluster + 1) * slot_cap)
        unit = jnp.concatenate(
            [
                jnp.concatenate(
                    [lines_ref[pl.ds(block * slots + slot, groups, stride=span), :] for slot in own_slots], axis=0
                ).astype(jnp.bfloat16)
                for block in range(features // LANES)
            ],
            axis=1,
        )
        products = lax.dot_general(unit, unit, dims, preferred_element_type=jnp.float32)
        rank_col = jnp.zeros((slot_cap * groups, 1), jnp.float32)
        rank_row = jnp.zeros((8, slot_cap * groups), jnp.float32)
        for digit in (high, low):
            own = jnp.concatenate([jnp.where(lane == slot, digit, 0.0) for slot in own_slots], axis=0)
            own = own.astype(jnp.bfloat16)
            rank_col += jnp.sum(own.astype(jnp.float32), axis=1, keepdims=True)
            rank_row += lax.dot_general(ones, own, dims, preferred_element_type=jnp.float32)
        rank_row = rank_row[0:1, :]
        rank_row = jnp.where(rank_row < DIGIT, jnp.float32(1e9), rank_row)
        allowed = rank_row < rank_col
        best = jnp.max(jnp.where(allowed, products, jnp.float32(-1.0)), axis=1, keepdims=True)
        for place, slot in enumerate(own_slots):
            best_lines = jnp.where(lane == slot, best[place * groups : (place + 1) * groups, :], best_lines)
    best_ref[...] = best_lines


def pick_kernel(slots, back_ref, slot_ref, out_ref):
    groups = back_ref.shape[0]
    rows = slot_ref.shape[1]
    ahead = slot_ref[...] - lax.broadcasted_iota(jnp.int32, (groups, rows), 0) * slots
    picked = jnp.zeros((groups, rows), jnp.float32)
    for slot in range(slots):
        picked = jnp.where(ahead == slot, back_ref[:, slot : slot + 1], picked)
    out_ref[...] = jnp.sum(picked, axis=0, keepdims=True)


def local(embeddings, cluster_ids, ranks):
    groups = lax.axis_size("grp")
    rows, features = embeddings.shape
    clusters = CLUS_DEV * groups
    slot_cap = 2 * rows // clusters
    slots = CLUS_DEV * slot_cap
    cluster_row = cluster_ids.reshape(1, rows)
    rank_row = ranks.reshape(1, rows)
    params = pltpu.CompilerParams(vmem_limit_bytes=48 * 1024 * 1024)

    def pack(*refs):
        pack_kernel(clusters, slot_cap, *refs)

    def score(*refs):
        score_kernel(slot_cap, groups, features, *refs)

    def pick(*refs):
        pick_kernel(slots, *refs)

    order = [
        [shard * groups + place for place in order_of_group(-1 if shard % 2 else 1)]
        for shard in range(lax.axis_size("shard"))
    ]

    def exchange(pieces):
        return lax.all_to_all(
            pieces, ("shard", "grp"), split_axis=0, concat_axis=0, axis_index_groups=order, tiled=True
        )

    span = lines_of(slots, features)
    lines = pltpu.VMEM((groups * span + 64, LANES), jnp.float32)
    send, slot_row = pl.pallas_call(
        pack,
        in_specs=[pl.BlockSpec(memory_space=pltpu.HBM)] * 3,
        out_shape=(
            jax.ShapeDtypeStruct((groups * span, LANES), jnp.bfloat16),
            jax.ShapeDtypeStruct((1, rows), jnp.int32),
        ),
        scratch_shapes=[
            pltpu.VMEM((rows, features), jnp.bfloat16),
            pltpu.VMEM((1, rows), jnp.int32),
            pltpu.VMEM((1, rows), jnp.int32),
            lines,
            pltpu.SemaphoreType.DMA((3,)),
        ],
        compiler_params=params,
        name="pack_rows",
    )(*(pltpu.with_memory_space_constraint(x, pltpu.HBM) for x in (embeddings, cluster_row, rank_row)))
    got = exchange(send.reshape(groups, span // 2, 2, LANES)).reshape(groups * span, LANES)
    best = pl.pallas_call(
        score,
        out_shape=jax.ShapeDtypeStruct((groups, LANES), jnp.float32),
        scratch_shapes=[lines],
        compiler_params=params,
        name="score_rows",
    )(got)
    back = exchange(best)
    out = pl.pallas_call(
        pick,
        out_shape=jax.ShapeDtypeStruct((1, rows), jnp.float32),
        compiler_params=params,
        name="pick_rows",
    )(back, slot_row)
    return out.reshape(rows)


def solution(mesh):
    in_specs = (P(("shard", "grp"), None), P(("shard", "grp"), None), P(("shard", "grp")))
    out_specs = P(("shard", "grp"))
    return jax.shard_map(local, mesh=mesh, in_specs=in_specs, out_specs=out_specs, check_vma=False)
```
